32 devices in a mesh: ctx: 8 (over z, y), fsdp: 4 (over x, core).
Axes of the slice: x: 2, y: 2, z: 4, core: 2. Of those that a mesh axis runs over, the one named last changes fastest.
Arguments:
- grad_out: bfloat16 [1024, 8192], P('ctx', 'fsdp'), may hold values from -6 to 6
- queries: bfloat16 [1024, 8192], P('ctx', 'fsdp'), may hold values from -6 to 6
- keys_in: bfloat16 [1024, 8192], P('ctx', 'fsdp'), may hold values from -6 to 6
- values_in: bfloat16 [1024, 8192], P('ctx', 'fsdp'), may hold values from -6 to 6
- filters: bfloat16 [512, 128], P('fsdp'), may hold values from -1.25 to 1.25
- out_weight: bfloat16 [8192, 8192], P('ctx', 'fsdp'), may hold values from -0.0625 to 0.0625
Outputs:
- grad_q: bfloat16 [1024, 8192], P('ctx', 'fsdp')
- grad_k: bfloat16 [1024, 8192], P('ctx', 'fsdp')
- grad_v: bfloat16 [1024, 8192], P('ctx', 'fsdp')
- grad_filters: float32 [512, 128], P('fsdp')
The draws below stay inside these ranges and needn't reach their ends.
All inputs are finite; a program needn't handle non-finite values.
Results may differ from the reference program's by a relative error of at most 0.015.
Values may be sent and summed in bfloat16 or wider, within the bound.
No kernel may reach another device: no remote copies, remote signals or barrier semaphores. Data moves between devices by JAX's collectives and lax.ppermute only.
A program may use at most 128 MiB of HBM per device.

```python
import jax
import jax.numpy as jnp
from jax import lax

D = 8192
G = 512
TAPS = 128
TOKENS = 1024


def block_levels(key, extent, split, least, top_value):
    def one(dim, parts):
        steps = jax.random.uniform(jax.random.fold_in(jax.random.fold_in(key, 6), dim), (parts,), jnp.float32, least / len(split), top_value / len(split))
        return jnp.repeat(jnp.exp(steps), extent[dim] // parts).reshape((-1,) + (1,) * (len(extent) - dim - 1))

    level = one(*split[0])
    for cut in split[1:]:
        level = level * one(*cut)
    return level


def normal_values(stream_key, dims, spread, bound, pieces=(), kind=jnp.bfloat16):
    array = spread * jax.random.normal(stream_key, dims, jnp.float32)
    if pieces:
        array = array * block_levels(stream_key, dims, pieces, -0.22, 0.18)
    return jnp.clip(array, -bound, bound).astype(kind)


def setup_inputs(seed: int = 0) -> dict:
    seeds = jax.random.split(jax.random.key(seed), 7)
    return {
        "grad_out": normal_values(seeds[0], (TOKENS, D), 1.0, 6.0, ((0, 8), (1, 4))),
        "queries": normal_values(seeds[1], (TOKENS, D), 1.0, 6.0, ((0, 8), (1, 4))),
        "keys_in": normal_values(seeds[2], (TOKENS, D), 1.0, 6.0, ((0, 8), (1, 4))),
        "values_in": normal_values(seeds[3], (TOKENS, D), 1.0, 6.0, ((0, 8), (1, 4))),
        "filters": normal_values(seeds[4], (G, TAPS), 0.09, 1.25, ((0, 4),)),
        "out_weight": normal_values(seeds[5], (D, D), D ** -0.5, 0.0625, ((0, 8), (1, 4))),
    }


def reference(grad_out, queries, keys_in, values_in, filters, out_weight):
    grad_y = jnp.dot(grad_out, out_weight, preferred_element_type=jnp.float32).astype(jnp.bfloat16)
    kvp = (keys_in.astype(jnp.float32) * values_in.astype(jnp.float32)).astype(jnp.bfloat16)
    kv_float = kvp.astype(jnp.float32)
    length = kv_float.shape[0]
    width = kv_float.shape[1]
    groups = filters.shape[0]
    taps = filters.shape[1]
    per_group = width // groups
    chan_filter = jnp.repeat(filters.astype(jnp.float32), per_group, axis=0).T
    kv_padded = jnp.concatenate([jnp.zeros((taps - 1, width), jnp.float32), kv_float], axis=0)

    def forward_tap(j, total):
        row = lax.dynamic_slice_in_dim(chan_filter, j, 1, 0)
        piece = lax.dynamic_slice_in_dim(kv_padded, taps - 1 - j, length, 0)
        return total + row * piece

    z_conv = lax.fori_loop(0, taps, forward_tap, jnp.zeros((length, width), jnp.float32))
    grad_yf = grad_y.astype(jnp.float32)
    grad_q = (grad_yf * z_conv).astype(jnp.bfloat16)
    grad_z = (grad_yf * queries.astype(jnp.float32)).astype(jnp.bfloat16)
    grad_zf = grad_z.astype(jnp.float32)
    gz_padded = jnp.concatenate([grad_zf, jnp.zeros((taps - 1, width), jnp.float32)], axis=0)

    def backward_tap(j, carry):
        total, rows = carry
        row = lax.dynamic_slice_in_dim(chan_filter, j, 1, 0)
        piece = lax.dynamic_slice_in_dim(gz_padded, j, length, 0)
        total = total + row * piece
        shifted = lax.dynamic_slice_in_dim(kv_padded, taps - 1 - j, length, 0)
        per_chan = jnp.sum(grad_zf * shifted, axis=0)
        per_group_sum = jnp.sum(per_chan.reshape(groups, per_group), axis=1)
        rows = lax.dynamic_update_slice_in_dim(rows, per_group_sum[None, :], j, 0)
        return total, rows

    grad_kv, filter_rows = lax.fori_loop(0, taps, backward_tap, (jnp.zeros((length, width), jnp.float32), jnp.zeros((taps, groups), jnp.float32)))
    grad_k = (grad_kv * values_in.astype(jnp.float32)).astype(jnp.bfloat16)
    grad_v = (grad_kv * keys_in.astype(jnp.float32)).astype(jnp.bfloat16)
    return grad_q, grad_k, grad_v, filter_rows.T
```

```python
import jax
import jax.numpy as jnp
from jax import lax
from jax.experimental import pallas as pl
from jax.experimental.pallas import tpu as pltpu
from jax.sharding import PartitionSpec as P

F32 = jnp.float32
BF16 = jnp.bfloat16
LANES = 128


def reversed_bits(value, count):
    out = 0
    for bit in range(count):
        out |= ((value >> bit) & 1) << (count - 1 - bit)
    return out


def traced_reversed_bits(value, count):
    out = jnp.zeros((), jnp.int32)
    for bit in range(count):
        out = out | (((value >> bit) & 1) << (count - 1 - bit))
    return out


def swap(block, axis, mask):
    size = lax.axis_size(axis)
    return lax.ppermute(block, axis, [(i, i ^ mask) for i in range(size)])


def from_behind(block, axis, distance):
    devices = range(lax.axis_size(axis))
    route = [(i - distance, i) for i in devices if i - distance in devices]
    return lax.ppermute(block, axis, route)


def lane_group(rows, per_group):
    return lax.broadcasted_iota(jnp.int32, (rows, LANES), 1) // per_group


def shifted_rows(row, taps, shift):
    wide = jnp.concatenate([row, jnp.zeros((1, taps), F32)], axis=1)
    return pltpu.roll(
        jnp.broadcast_to(wide, (taps, 2 * taps)), shift, 1, stride=1, stride_axis=0
    )


def pick_groups(stacked, taps, per_group):
    groups = LANES // per_group
    lane = lane_group(taps, per_group)
    out = stacked[:taps]
    for g in range(1, groups):
        out = jnp.where(lane == g, stacked[g * taps : (g + 1) * taps], out)
    return out


def make_before_kernel(taps, per_group):
    groups = LANES // per_group

    def kernel(f_ref, frev_ref, kvp_ref, prior_ref, z_ref, near_ref, far_ref, kvrev_ref):
        kv = jnp.concatenate([prior_ref[...], kvp_ref[...]], axis=0)
        rows = []
        for g in range(groups):
            toe = shifted_rows(frev_ref[g : g + 1, :], taps, 1)
            rows.append(toe.astype(BF16))
            back = shifted_rows(f_ref[g : g + 1, :], taps, 0).astype(BF16)
            near_ref[g * taps : (g + 1) * taps, :] = back[:, :taps]
            far_ref[g * taps : (g + 1) * taps, :] = back[:, taps:]
        stacked = jnp.dot(jnp.concatenate(rows, axis=0), kv, preferred_element_type=F32)
        z_ref[...] = pick_groups(stacked, taps, per_group)
        r = lax.broadcasted_iota(jnp.int32, (2 * taps, 2 * taps), 0)
        c = lax.broadcasted_iota(jnp.int32, (2 * taps, 2 * taps), 1)
        flip = jnp.where(r + c == 2 * taps - 1, 1.0, 0.0).astype(BF16)
        kvrev_ref[...] = jnp.dot(flip, kv, preferred_element_type=F32).astype(BF16)

    return kernel


def make_pair_kernel(taps, per_group):
    groups = LANES // per_group

    def kernel(gz_ref, near_ref, kvrev_ref, own_ref, gf_ref):
        gz = gz_ref[...]
        stacked = jnp.dot(near_ref[...], gz, preferred_element_type=F32)
        own_ref[...] = pick_groups(stacked, taps, per_group)
        lane = lane_group(taps, per_group)
        kvrev = kvrev_ref[...]
        zero = jnp.zeros_like(gz)
        for g in range(groups):
            pair = lax.dot_general(
                jnp.where(lane == g, gz, zero),
                kvrev,
                (((1,), (1,)), ((), ())),
                preferred_element_type=F32,
            )
            rolled = pltpu.roll(pair, taps + 1, 1, stride=1, stride_axis=0)
            gf_ref[g : g + 1, :] = jnp.sum(rolled[:, :taps], axis=0, keepdims=True)

    return kernel


def make_after_kernel(taps, per_group):
    def kernel(later_ref, far_ref, own_ref, k_ref, v_ref, gk_ref, gv_ref):
        stacked = jnp.dot(far_ref[...], later_ref[...], preferred_element_type=F32)
        grad_kv = own_ref[...] + pick_groups(stacked, taps, per_group)
        gk_ref[...] = (grad_kv * v_ref[...].astype(F32)).astype(BF16)
        gv_ref[...] = (grad_kv * k_ref[...].astype(F32)).astype(BF16)

    return kernel


def gather_features(grad_out, rows_here):
    n = lax.axis_size("ctx")
    nf = lax.axis_size("fsdp")
    r = n // nf
    bits = nf.bit_length() - 1
    mine = lax.axis_index("ctx")
    pieces = []
    for e in reversed(range(r)):
        route = []
        for i in range(n):
            for dj in range(nf):
                source = i ^ (r * dj + e)
                target = i * nf + reversed_bits(dj, bits)
                route.append((source * nf + i // r, target))
        part = (mine % r) ^ e
        cut = lax.dynamic_slice_in_dim(grad_out, part * rows_here, rows_here, axis=1)
        got = lax.ppermute(cut, ("ctx", "fsdp"), route)
        pieces.append((e, got[None]))
    out = {}
    for e, held in pieces:
        for bit in reversed(range(bits)):
            held = jnp.concatenate([held, swap(held, "fsdp", 1 << bit)], axis=0)
        out[e] = held
    return out


def per_device(grad_out, queries, keys_in, values_in, filters, out_weight):
    n = lax.axis_size("ctx")
    nf = lax.axis_size("fsdp")
    r = n // nf
    bits = nf.bit_length() - 1
    tokens_here, channels = grad_out.shape
    group_count, taps = filters.shape
    per_group = channels // group_count
    groups = LANES // per_group
    octets = channels // LANES
    rows_here = out_weight.shape[0]

    held = gather_features(grad_out, rows_here)
    column = lax.axis_index("fsdp")

    def block(d):
        dj, e = d // r, d % r
        q = reversed_bits(dj, bits) ^ column
        place = traced_reversed_bits(q, bits)
        return lax.dynamic_index_in_dim(held[e], place, 0, keepdims=False)

    kvp = (keys_in.astype(F32) * values_in.astype(F32)).astype(BF16)
    prior = from_behind(kvp, "ctx", 1)

    def partial(blocks):
        lhs = jnp.concatenate([block(d) for d in blocks], axis=0)
        return jnp.dot(lhs, out_weight, preferred_element_type=F32)

    half = max(n // 2, 2)
    sums = {}
    for first in (half, 0):
        odd = [d for d in range(first, first + n // 2) if d & 1]
        even = [d for d in range(first, first + n // 2) if not d & 1]
        sent = swap(partial(odd).astype(BF16), "ctx", 1).astype(F32)
        total = partial(even) + sent
        for at, d in enumerate(even):
            sums[d] = total[at * tokens_here : (at + 1) * tokens_here]
    stage = 2
    while stage < n:
        for d in sorted((d for d in sums if d & stage), reverse=True):
            got = swap(sums.pop(d).astype(BF16), "ctx", stage)
            sums[d ^ stage] = sums[d ^ stage] + got.astype(F32)
        stage *= 2
    grad_y = sums[0].astype(BF16).astype(F32)

    filters32 = filters.astype(F32)
    lane_block = pl.BlockSpec((tokens_here, LANES), lambda o: (0, o))
    filter_block = pl.BlockSpec((groups, taps), lambda o: (o, 0))
    toe_block = pl.BlockSpec((groups * taps, taps), lambda o: (o, 0))
    ext_block = pl.BlockSpec((2 * tokens_here, LANES), lambda o: (0, o))
    toe_shape = jax.ShapeDtypeStruct((group_count * taps, taps), BF16)
    plane32 = jax.ShapeDtypeStruct((tokens_here, channels), F32)
    plane16 = jax.ShapeDtypeStruct((tokens_here, channels), BF16)
    macs = channels * taps * tokens_here * groups
    z_conv, near, far, kvrev = pl.pallas_call(
        make_before_kernel(taps, per_group),
        grid=(octets,),
        in_specs=[filter_block, filter_block, lane_block, lane_block],
        out_specs=[lane_block, toe_block, toe_block, ext_block],
        out_shape=[
            plane32,
            toe_shape,
            toe_shape,
            jax.ShapeDtypeStruct((2 * tokens_here, channels), BF16),
        ],
        cost_estimate=pl.CostEstimate(flops=4 * macs, bytes_accessed=24 << 20, transcendentals=0),
        name="forward_conv",
    )(filters32, filters32[:, ::-1], kvp, prior)

    grad_q = (grad_y * z_conv).astype(BF16)
    grad_z = (grad_y * queries.astype(F32)).astype(BF16)
    later = from_behind(grad_z, "ctx", -1)

    own, local_terms = pl.pallas_call(
        make_pair_kernel(taps, per_group),
        grid=(octets,),
        in_specs=[lane_block, toe_block, ext_block],
        out_specs=[lane_block, filter_block],
        out_shape=[plane32, jax.ShapeDtypeStruct((group_count, taps), F32)],
        cost_estimate=pl.CostEstimate(flops=4 * macs, bytes_accessed=12 << 20, transcendentals=0),
        name="pair_products",
    )(grad_z, near, kvrev)
    grad_filters = local_terms
    stage = 1
    while stage < n:
        grad_filters = grad_filters + swap(grad_filters, "ctx", stage)
        stage *= 2

    grad_k, grad_v = pl.pallas_call(
        make_after_kernel(taps, per_group),
        grid=(octets,),
        in_specs=[lane_block, toe_block, lane_block, lane_block, lane_block],
        out_specs=[lane_block, lane_block],
        out_shape=[plane16, plane16],
        cost_estimate=pl.CostEstimate(flops=2 * macs, bytes_accessed=8 << 20, transcendentals=0),
        name="backward_conv",
    )(later, far, own, keys_in, values_in)
    return (grad_q, grad_k, grad_v, grad_filters)


def solution(mesh):
    placed = (
        P("ctx", "fsdp"),
        P("ctx", "fsdp"),
        P("ctx", "fsdp"),
        P("ctx", "fsdp"),
        P("fsdp", None),
        P("ctx", "fsdp"),
    )
    return jax.shard_map(
        per_device,
        mesh=mesh,
        in_specs=placed,
        out_specs=(P("ctx", "fsdp"), P("ctx", "fsdp"), P("ctx", "fsdp"), P("fsdp", None)),
        check_vma=False,
    )
```

```python
import jax
import jax.numpy as jnp
from jax import lax
from jax.experimental import pallas as pl
from jax.experimental.pallas import tpu as pltpu
from jax.sharding import PartitionSpec as P

F32 = jnp.float32
BF16 = jnp.bfloat16
LANES = 128
PARTS = 1
KQ = 9
ZQ = 2
DET = True
DIRECT = 3
ROWS = 32


def reversed_bits(value, count):
    out = 0
    for bit in range(count):
        out |= ((value >> bit) & 1) << (count - 1 - bit)
    return out


def swap(block, axis, mask):
    size = lax.axis_size(axis)
    return lax.ppermute(block, axis, [(i, i ^ mask) for i in range(size)])


def from_behind(block, axis, distance):
    devices = range(lax.axis_size(axis))
    route = [(i - distance, i) for i in devices if i - distance in devices]
    return lax.ppermute(block, axis, route)


def lane_group(rows, per_group):
    return lax.broadcasted_iota(jnp.int32, (rows, LANES), 1) // per_group


def shifted_rows(row, taps, shift):
    wide = jnp.concatenate([row, jnp.zeros((1, taps), F32)], axis=1)
    return pltpu.roll(
        jnp.broadcast_to(wide, (taps, 2 * taps)), shift, 1, stride=1, stride_axis=0
    )


def pick_groups(stacked, taps, per_group):
    groups = LANES // per_group
    lane = lane_group(taps, per_group)
    out = stacked[:taps]
    for g in range(1, groups):
        out = jnp.where(lane == g, stacked[g * taps : (g + 1) * taps], out)
    return out


def make_before_kernel(taps, per_group, octets):
    groups = LANES // per_group

    def kernel(f_ref, frev_ref, kvp_ref, prior_ref, z_ref, toe_ref, kvrev_ref):
        r = lax.broadcasted_iota(jnp.int32, (2 * taps, 2 * taps), 0)
        c = lax.broadcasted_iota(jnp.int32, (2 * taps, 2 * taps), 1)
        flip = jnp.where(r + c == 2 * taps - 1, 1.0, 0.0).astype(BF16)
        for o in range(octets):
            lanes = slice(o * LANES, (o + 1) * LANES)
            kv = jnp.concatenate([prior_ref[:, lanes], kvp_ref[:, lanes]], axis=0)
            rows = []
            for g in range(o * groups, (o + 1) * groups):
                toe = shifted_rows(frev_ref[g : g + 1, :], taps, 1)
                rows.append(toe.astype(BF16))
                back = shifted_rows(f_ref[g : g + 1, :], taps, 0).astype(BF16)
                toe_ref[g * taps : (g + 1) * taps, :] = back
            stacked = jnp.dot(jnp.concatenate(rows, axis=0), kv, preferred_element_type=F32)
            z_ref[:, lanes] = pick_groups(stacked, taps, per_group)
            kvrev_ref[: taps - ROWS, lanes] = jnp.zeros((taps - ROWS, LANES), BF16)
            kvrev_ref[taps - ROWS :, lanes] = jnp.dot(flip, kv, preferred_element_type=F32).astype(BF16)

    return kernel


def make_pair_kernel(taps, per_group, octets):
    groups = LANES // per_group

    def kernel(gz_ref, kvrev_ref, gf_ref):
        lane = lane_group(taps, per_group)
        for o in range(octets):
            lanes = slice(o * LANES, (o + 1) * LANES)
            gz = gz_ref[:, lanes]
            zero = jnp.zeros((ROWS, LANES), BF16)
            pairs = None
            for at in range(0, taps, ROWS):
                rows = gz[at : at + ROWS]
                split = [jnp.where(lane[:ROWS] == g, rows, zero) for g in range(groups)]
                start = taps - ROWS - at
                term = lax.dot_general(
                    jnp.concatenate(split, axis=0),
                    kvrev_ref[start : start + 2 * taps, lanes],
                    (((1,), (1,)), ((), ())),
                    preferred_element_type=F32,
                )
                pairs = term if pairs is None else pairs + term
            for g in range(groups):
                pair = pairs[g * ROWS : (g + 1) * ROWS]
                rolled = pltpu.roll(pair, taps + 1, 1, stride=1, stride_axis=0)
                row = o * groups + g
                gf_ref[row : row + 1, :] = jnp.sum(rolled[:, :taps], axis=0, keepdims=True)

    return kernel


def make_after_kernel(taps, per_group, octets):
    groups = LANES // per_group

    def kernel(gz_ref, later_ref, toe_ref, k_ref, v_ref, *refs):
        gk_ref, gv_ref = refs[-2:]
        for o in range(octets):
            lanes = slice(o * LANES, (o + 1) * LANES)
            toes = slice(o * groups * taps, (o + 1) * groups * taps)
            ext = jnp.concatenate([gz_ref[:, lanes], later_ref[:, lanes]], axis=0)
            stacked = jnp.dot(toe_ref[toes, :], ext, preferred_element_type=F32)
            grad_kv = pick_groups(stacked, taps, per_group)
            gk_ref[:, lanes] = (grad_kv * v_ref[:, lanes].astype(F32)).astype(BF16)
            gv_ref[:, lanes] = (grad_kv * k_ref[:, lanes].astype(F32)).astype(BF16)

    return kernel


def first_piece(grad_out, rows_here, e):
    n = lax.axis_size("ctx")
    nf = lax.axis_size("fsdp")
    r = n // nf
    bits = nf.bit_length() - 1
    mine = lax.axis_index("ctx")
    detour = nf // 2 if DET and (r - 1 - e) % 2 else 0
    route = []
    for i in range(n):
        for dj in range(nf):
            source = i ^ (r * dj + e)
            target = i * nf + reversed_bits(dj, bits)
            route.append((source * nf + ((i // r) ^ detour), target))
    part = (mine % r) ^ e
    cut = lax.dynamic_slice_in_dim(grad_out, part * rows_here, rows_here, axis=1)
    if detour:
        cut = swap(cut, "fsdp", detour)
    return lax.ppermute(cut, ("ctx", "fsdp"), route)


def block_before(kvp):
    n = lax.axis_size("ctx")
    mine = lax.axis_index("ctx")
    near = swap(kvp, "ctx", 1)
    far = lax.ppermute(near, "ctx", [(i, i + 2) for i in range(0, n - 2, 2)])
    return jnp.where(mine % 2 == 1, near, far)


def to_owner(block, q):
    n = lax.axis_size("ctx")
    nf = lax.axis_size("fsdp")
    r = n // nf
    bits = nf.bit_length() - 1
    route = []
    for i in range(n):
        for j in range(nf):
            dj = reversed_bits(j ^ q, bits)
            route.append((i * nf + j, (i ^ (r * dj)) * nf + j))
    return lax.ppermute(block, ("ctx", "fsdp"), route)


def tree_sum(values):
    while len(values) > 1:
        values = [a + b for a, b in zip(values[::2], values[1::2])]
    return values[0]


def summed_over_ctx(value, after):
    n = lax.axis_size("ctx")
    stride = 1
    while stride < n:
        reach = min(DIRECT + 1, n // stride)
        sent = value.astype(BF16)
        got = [swap(sent, "ctx", k * stride) for k in range(1, reach)]
        stride *= reach
        if stride >= n:
            got, after = lax.optimization_barrier((got, after))
        value = tree_sum([each.astype(F32) for each in [sent] + got])
    return value, after


def per_device(grad_out, queries, keys_in, values_in, filters, out_weight):
    n = lax.axis_size("ctx")
    nf = lax.axis_size("fsdp")
    r = n // nf
    tokens_here, channels = grad_out.shape
    group_count, taps = filters.shape
    per_group = channels // group_count
    groups = LANES // per_group
    octets = channels // LANES
    rows_here = out_weight.shape[0]
    parts = min(PARTS, octets)
    width = channels // parts
    per_part = octets // parts
    per_step = min(per_part, 4)
    steps = per_part // per_step

    kvp = (keys_in.astype(F32) * values_in.astype(F32)).astype(BF16)
    held = {"prior": block_before(kvp)}
    pieces = {}
    for e in reversed(range(r)):
        pieces[0, e] = first_piece(grad_out, rows_here, e)
        for q in range(1, nf):
            low = q & -q
            pieces[q, e] = swap(pieces[q ^ low, e], "fsdp", low)

    filters32 = filters.astype(F32)
    ext_rows = 3 * taps - ROWS
    lane_block = pl.BlockSpec((tokens_here, per_step * LANES), lambda o: (0, o))
    filter_block = pl.BlockSpec((per_step * groups, taps), lambda o: (o, 0))
    toe_block = pl.BlockSpec((per_step * groups * taps, 2 * taps), lambda o: (o, 0))
    ext_block = pl.BlockSpec((ext_rows, per_step * LANES), lambda o: (0, o))
    macs = channels * taps * tokens_here * groups
    params = pltpu.CompilerParams(vmem_limit_bytes=40 << 20)
    def block_sum(q, cols, earlier):
        weight = out_weight[:, cols]
        sums = {e: jnp.dot(pieces[q, e], weight, preferred_element_type=F32) for e in range(r)}
        bit = 1
        while bit < r:
            for e in [e for e in sums if e & bit]:
                got = swap(sums.pop(e).astype(BF16), "ctx", bit)
                if len(earlier) == KQ:
                    got, held["prior"] = lax.optimization_barrier((got, held["prior"]))
                if len(earlier) == ZQ:
                    got, earlier[0] = lax.optimization_barrier((got, earlier[0]))
                sums[e ^ bit] = sums[e ^ bit] + got.astype(F32)
            bit *= 2
        return to_owner(sums[0].astype(BF16), q)

    whole_blocks = []
    for q in range(nf - 1):
        whole_blocks.append(block_sum(q, slice(0, channels), whole_blocks))
    z_conv, toes, kvrev = pl.pallas_call(
        make_before_kernel(taps, per_group, per_step),
        grid=(octets // per_step,),
        in_specs=[filter_block, filter_block, lane_block, lane_block],
        out_specs=[lane_block, toe_block, ext_block],
        out_shape=[
            jax.ShapeDtypeStruct((tokens_here, channels), F32),
            jax.ShapeDtypeStruct((group_count * taps, 2 * taps), BF16),
            jax.ShapeDtypeStruct((ext_rows, channels), BF16),
        ],
        compiler_params=params,
        cost_estimate=pl.CostEstimate(flops=4 * macs, bytes_accessed=24 << 20, transcendentals=0),
        name="forward_conv",
    )(filters32, filters32[:, ::-1], kvp, held["prior"])

    grad_qs, terms = [], []
    grad_k = grad_v = None
    for part in range(parts):
        cols = slice(part * width, (part + 1) * width)
        owned = [block[:, cols] for block in whole_blocks] + [block_sum(nf - 1, cols, whole_blocks)]
        grad_y = sum(block.astype(F32) for block in owned).astype(BF16).astype(F32)
        grad_qs.append((grad_y * z_conv[:, cols]).astype(BF16))
        grad_z = (grad_y * queries[:, cols].astype(F32)).astype(BF16)
        later = from_behind(grad_z, "ctx", -1)

        base = part * steps
        part_lanes = pl.BlockSpec((tokens_here, per_step * LANES), lambda o, b=base: (0, o + b))
        part_toes = pl.BlockSpec((per_step * groups * taps, 2 * taps), lambda o, b=base: (o + b, 0))
        part_ext = pl.BlockSpec((ext_rows, per_step * LANES), lambda o, b=base: (0, o + b))
        local_terms = pl.pallas_call(
            make_pair_kernel(taps, per_group, per_step),
            grid=(steps,),
            in_specs=[lane_block, part_ext],
            out_specs=filter_block,
            out_shape=jax.ShapeDtypeStruct((group_count // parts, taps), F32),
            compiler_params=params,
            cost_estimate=pl.CostEstimate(
                flops=4 * macs // parts, bytes_accessed=(12 << 20) // parts, transcendentals=0
            ),
            name="pair_products",
        )(grad_z, kvrev)
        terms.append(local_terms)

        earlier = [] if part == 0 else [grad_k, grad_v]
        plane16 = jax.ShapeDtypeStruct((tokens_here, channels), BF16)
        grad_k, grad_v = pl.pallas_call(
            make_after_kernel(taps, per_group, per_step),
            grid=(steps,),
            in_specs=[lane_block, lane_block, part_toes, part_lanes, part_lanes]
            + [pl.BlockSpec(memory_space=pl.ANY)] * len(earlier),
            out_specs=[part_lanes, part_lanes],
            out_shape=[plane16, plane16],
            input_output_aliases={5 + at: at for at in range(len(earlier))},
            compiler_params=params,
            cost_estimate=pl.CostEstimate(
                flops=2 * macs // parts, bytes_accessed=(8 << 20) // parts, transcendentals=0
            ),
            name="backward_conv",
        )(grad_z, later, toes, keys_in, values_in, *earlier)

    grad_filters, (grad_k, grad_v) = summed_over_ctx(jnp.concatenate(terms, axis=0), (grad_k, grad_v))
    return (jnp.concatenate(grad_qs, axis=1), grad_k, grad_v, grad_filters)


def solution(mesh):
    placed = (
        P("ctx", "fsdp"),
        P("ctx", "fsdp"),
        P("ctx", "fsdp"),
        P("ctx", "fsdp"),
        P("fsdp", None),
        P("ctx", "fsdp"),
    )
    return jax.shard_map(
        per_device,
        mesh=mesh,
        in_specs=placed,
        out_specs=(P("ctx", "fsdp"), P("ctx", "fsdp"), P("ctx", "fsdp"), P("fsdp", None)),
        check_vma=False,
    )
```

```python
import jax
import jax.numpy as jnp
from jax import lax
from jax.experimental import pallas as pl
from jax.experimental.pallas import tpu as pltpu
from jax.sharding import PartitionSpec as P

F32 = jnp.float32
BF16 = jnp.bfloat16
LANES = 128
PARTS = 1
FLIGHT = 2
KQ = 1
CUTX = False
ZQ = 2
DET = True
ROWS = 32


def reversed_bits(value, count):
    out = 0
    for bit in range(count):
        out |= ((value >> bit) & 1) << (count - 1 - bit)
    return out


def swap(block, axis, mask):
    size = lax.axis_size(axis)
    return lax.ppermute(block, axis, [(i, i ^ mask) for i in range(size)])


def from_behind(block, axis, distance):
    devices = range(lax.axis_size(axis))
    route = [(i - distance, i) for i in devices if i - distance in devices]
    return lax.ppermute(block, axis, route)


def lane_group(rows, per_group):
    return lax.broadcasted_iota(jnp.int32, (rows, LANES), 1) // per_group


def shifted_rows(row, taps, shift):
    wide = jnp.concatenate([row, jnp.zeros((1, taps), F32)], axis=1)
    return pltpu.roll(
        jnp.broadcast_to(wide, (taps, 2 * taps)), shift, 1, stride=1, stride_axis=0
    )


def pick_groups(stacked, taps, per_group):
    groups = LANES // per_group
    lane = lane_group(taps, per_group)
    out = stacked[:taps]
    for g in range(1, groups):
        out = jnp.where(lane == g, stacked[g * taps : (g + 1) * taps], out)
    return out


def product_kernel(k_ref, v_ref, kvp_ref):
    kvp_ref[...] = (k_ref[...].astype(F32) * v_ref[...].astype(F32)).astype(BF16)


def make_before_kernel(taps, per_group, octets):
    groups = LANES // per_group

    def kernel(f_ref, frev_ref, kvp_ref, prior_ref, z_ref, toe_ref, kvrev_ref):
        r = lax.broadcasted_iota(jnp.int32, (2 * taps, 2 * taps), 0)
        c = lax.broadcasted_iota(jnp.int32, (2 * taps, 2 * taps), 1)
        flip = jnp.where(r + c == 2 * taps - 1, 1.0, 0.0).astype(BF16)
        for o in range(octets):
            lanes = slice(o * LANES, (o + 1) * LANES)
            kv = jnp.concatenate([prior_ref[:, lanes], kvp_ref[:, lanes]], axis=0)
            rows = []
            for g in range(o * groups, (o + 1) * groups):
                toe = shifted_rows(frev_ref[g : g + 1, :], taps, 1)
                rows.append(toe.astype(BF16))
                back = shifted_rows(f_ref[g : g + 1, :], taps, 0).astype(BF16)
                toe_ref[g * taps : (g + 1) * taps, :] = back
            stacked = jnp.dot(jnp.concatenate(rows, axis=0), kv, preferred_element_type=F32)
            z_ref[:, lanes] = pick_groups(stacked, taps, per_group)
            kvrev_ref[: taps - ROWS, lanes] = jnp.zeros((taps - ROWS, LANES), BF16)
            kvrev_ref[taps - ROWS :, lanes] = jnp.dot(flip, kv, preferred_element_type=F32).astype(BF16)

    return kernel


def make_pair_kernel(taps, per_group, octets):
    groups = LANES // per_group

    def kernel(gz_ref, kvrev_ref, gf_ref):
        lane = lane_group(taps, per_group)
        for o in range(octets):
            lanes = slice(o * LANES, (o + 1) * LANES)
            gz = gz_ref[:, lanes]
            zero = jnp.zeros((ROWS, LANES), BF16)
            pairs = None
            for at in range(0, taps, ROWS):
                rows = gz[at : at + ROWS]
                split = [jnp.where(lane[:ROWS] == g, rows, zero) for g in range(groups)]
                start = taps - ROWS - at
                term = lax.dot_general(
                    jnp.concatenate(split, axis=0),
                    kvrev_ref[start : start + 2 * taps, lanes],
                    (((1,), (1,)), ((), ())),
                    preferred_element_type=F32,
                )
                pairs = term if pairs is None else pairs + term
            for g in range(groups):
                pair = pairs[g * ROWS : (g + 1) * ROWS]
                rolled = pltpu.roll(pair, taps + 1, 1, stride=1, stride_axis=0)
                row = o * groups + g
                gf_ref[row : row + 1, :] = jnp.sum(rolled[:, :taps], axis=0, keepdims=True)

    return kernel


def make_after_kernel(taps, per_group, octets):
    groups = LANES // per_group

    def kernel(gz_ref, later_ref, toe_ref, k_ref, v_ref, *refs):
        gk_ref, gv_ref = refs[-2:]
        for o in range(octets):
            lanes = slice(o * LANES, (o + 1) * LANES)
            toes = slice(o * groups * taps, (o + 1) * groups * taps)
            ext = jnp.concatenate([gz_ref[:, lanes], later_ref[:, lanes]], axis=0)
            stacked = jnp.dot(toe_ref[toes, :], ext, preferred_element_type=F32)
            grad_kv = pick_groups(stacked, taps, per_group)
            gk_ref[:, lanes] = (grad_kv * v_ref[:, lanes].astype(F32)).astype(BF16)
            gv_ref[:, lanes] = (grad_kv * k_ref[:, lanes].astype(F32)).astype(BF16)

    return kernel


def first_piece(grad_out, rows_here, e):
    n = lax.axis_size("ctx")
    nf = lax.axis_size("fsdp")
    r = n // nf
    bits = nf.bit_length() - 1
    mine = lax.axis_index("ctx")
    detour = nf // 2 if DET and (r - 1 - e) % 2 else 0
    route = []
    for i in range(n):
        for dj in range(nf):
            source = i ^ (r * dj + e)
            target = i * nf + reversed_bits(dj, bits)
            route.append((source * nf + ((i // r) ^ detour), target))
    part = (mine % r) ^ e
    cut = lax.dynamic_slice_in_dim(grad_out, part * rows_here, rows_here, axis=1)
    if detour:
        cut = swap(cut, "fsdp", detour)
    return cut, lax.ppermute(cut, ("ctx", "fsdp"), route)


def to_owner(block, q):
    n = lax.axis_size("ctx")
    nf = lax.axis_size("fsdp")
    r = n // nf
    bits = nf.bit_length() - 1
    route = []
    for i in range(n):
        for j in range(nf):
            dj = reversed_bits(j ^ q, bits)
            route.append((i * nf + j, (i ^ (r * dj)) * nf + j))
    return lax.ppermute(block, ("ctx", "fsdp"), route)


def tree_sum(values):
    while len(values) > 1:
        values = [a + b for a, b in zip(values[::2], values[1::2])]
    return values[0]


def summed_over_ctx(value, halo, after):
    n = lax.axis_size("ctx")
    steps = []
    at = 2
    while at < n:
        steps.append([k * at for k in (1, 2, 3) if k * at < n])
        at *= 4
    steps.append([1])
    for step in steps:
        sent = value.astype(BF16)
        if step == [1]:
            sent, halo = lax.optimization_barrier((sent, halo))
        got = [swap(sent, "ctx", mask) for mask in step]
        if step == [1]:
            got, after = lax.optimization_barrier((got, after))
        value = tree_sum([each.astype(F32) for each in [sent] + got])
    return value, after


def per_device(grad_out, queries, keys_in, values_in, filters, out_weight):
    n = lax.axis_size("ctx")
    nf = lax.axis_size("fsdp")
    r = n // nf
    tokens_here, channels = grad_out.shape
    group_count, taps = filters.shape
    per_group = channels // group_count
    groups = LANES // per_group
    octets = channels // LANES
    rows_here = out_weight.shape[0]
    parts = min(PARTS, octets)
    width = channels // parts
    per_part = octets // parts
    per_step = min(per_part, 8)
    steps = per_part // per_step

    kvp = pl.pallas_call(
        product_kernel,
        out_shape=jax.ShapeDtypeStruct((tokens_here, channels), BF16),
        cost_estimate=pl.CostEstimate(flops=1 << 20, bytes_accessed=64 << 20, transcendentals=0),
        name="kv_product",
    )(keys_in, values_in)
    arrived = []
    held = {"prior": from_behind(kvp, "ctx", 1)}
    pieces = {}
    cuts = {}
    for e in range(r):
        cuts[e], pieces[0, e] = first_piece(grad_out, rows_here, e)
    for e in range(r):
        for q in range(1, nf):
            low = q & -q
            piece = pieces[q ^ low, e]
            if CUTX and r > 1 and e == r - 1 and q == nf // 2:
                piece, cuts[0] = lax.optimization_barrier((piece, cuts[0]))
            pieces[q, e] = swap(piece, "fsdp", low)

    filters32 = filters.astype(F32)
    ext_rows = 3 * taps - ROWS
    lane_block = pl.BlockSpec((tokens_here, per_step * LANES), lambda o: (0, o))
    filter_block = pl.BlockSpec((per_step * groups, taps), lambda o: (o, 0))
    toe_block = pl.BlockSpec((per_step * groups * taps, 2 * taps), lambda o: (o, 0))
    ext_block = pl.BlockSpec((ext_rows, per_step * LANES), lambda o: (0, o))
    macs = channels * taps * tokens_here * groups
    params = pltpu.CompilerParams(vmem_limit_bytes=40 << 20)
    def block_sum(q, cols, earlier):
        weight = out_weight[:, cols]
        sums = {e: jnp.dot(pieces[q, e], weight, preferred_element_type=F32) for e in range(r)}
        bit = 1
        while bit < r:
            for e in [e for e in sums if e & bit]:
                sent = sums.pop(e).astype(BF16)
                if len(arrived) >= FLIGHT:
                    sent, arrived[-FLIGHT] = lax.optimization_barrier((sent, arrived[-FLIGHT]))
                got = swap(sent, "ctx", bit)
                if len(earlier) == KQ:
                    got, held["prior"] = lax.optimization_barrier((got, held["prior"]))
                arrived.append(got)
                if len(earlier) == ZQ:
                    got, earlier[0] = lax.optimization_barrier((got, earlier[0]))
                sums[e ^ bit] = sums[e ^ bit] + got.astype(F32)
            bit *= 2
        return to_owner(sums[0].astype(BF16), q)

    whole_blocks = []
    for q in range(nf - 1):
        whole_blocks.append(block_sum(q, slice(0, channels), whole_blocks))
    last_blocks = []
    for part in range(parts):
        cols = slice(part * width, (part + 1) * width)
        last_blocks.append(block_sum(nf - 1, cols, whole_blocks))
    prior = held["prior"]

    z_conv, toes, kvrev = pl.pallas_call(
        make_before_kernel(taps, per_group, per_step),
        grid=(octets // per_step,),
        in_specs=[filter_block, filter_block, lane_block, lane_block],
        out_specs=[lane_block, toe_block, ext_block],
        out_shape=[
            jax.ShapeDtypeStruct((tokens_here, channels), F32),
            jax.ShapeDtypeStruct((group_count * taps, 2 * taps), BF16),
            jax.ShapeDtypeStruct((ext_rows, channels), BF16),
        ],
        compiler_params=params,
        cost_estimate=pl.CostEstimate(flops=4 * macs, bytes_accessed=24 << 20, transcendentals=0),
        name="forward_conv",
    )(filters32, filters32[:, ::-1], kvp, prior)

    grad_qs, terms = [], []
    grad_k = grad_v = None
    for part in range(parts):
        cols = slice(part * width, (part + 1) * width)
        owned = [block[:, cols] for block in whole_blocks] + [last_blocks[part]]
        grad_y = sum(block.astype(F32) for block in owned).astype(BF16).astype(F32)
        grad_qs.append((grad_y * z_conv[:, cols]).astype(BF16))
        grad_z = (grad_y * queries[:, cols].astype(F32)).astype(BF16)
        later = from_behind(grad_z, "ctx", -1)

        base = part * steps
        part_lanes = pl.BlockSpec((tokens_here, per_step * LANES), lambda o, b=base: (0, o + b))
        part_toes = pl.BlockSpec((per_step * groups * taps, 2 * taps), lambda o, b=base: (o + b, 0))
        part_ext = pl.BlockSpec((ext_rows, per_step * LANES), lambda o, b=base: (0, o + b))
        local_terms = pl.pallas_call(
            make_pair_kernel(taps, per_group, per_step),
            grid=(steps,),
            in_specs=[lane_block, part_ext],
            out_specs=filter_block,
            out_shape=jax.ShapeDtypeStruct((group_count // parts, taps), F32),
            compiler_params=params,
            cost_estimate=pl.CostEstimate(
                flops=4 * macs // parts, bytes_accessed=(12 << 20) // parts, transcendentals=0
            ),
            name="pair_products",
        )(grad_z, kvrev)
        terms.append(local_terms)

        earlier = [] if part == 0 else [grad_k, grad_v]
        plane16 = jax.ShapeDtypeStruct((tokens_here, channels), BF16)
        grad_k, grad_v = pl.pallas_call(
            make_after_kernel(taps, per_group, per_step),
            grid=(steps,),
            in_specs=[lane_block, lane_block, part_toes, part_lanes, part_lanes]
            + [pl.BlockSpec(memory_space=pl.ANY)] * len(earlier),
            out_specs=[part_lanes, part_lanes],
            out_shape=[plane16, plane16],
            input_output_aliases={5 + at: at for at in range(len(earlier))},
            compiler_params=params,
            cost_estimate=pl.CostEstimate(
                flops=2 * macs // parts, bytes_accessed=(8 << 20) // parts, transcendentals=0
            ),
            name="backward_conv",
        )(grad_z, later, toes, keys_in, values_in, *earlier)

    grad_filters, (grad_k, grad_v) = summed_over_ctx(jnp.concatenate(terms, axis=0), later, (grad_k, grad_v))
    return (jnp.concatenate(grad_qs, axis=1), grad_k, grad_v, grad_filters)


def solution(mesh):
    placed = (
        P("ctx", "fsdp"),
        P("ctx", "fsdp"),
        P("ctx", "fsdp"),
        P("ctx", "fsdp"),
        P("fsdp", None),
        P("ctx", "fsdp"),
    )
    return jax.shard_map(
        per_device,
        mesh=mesh,
        in_specs=placed,
        out_specs=(P("ctx", "fsdp"), P("ctx", "fsdp"), P("ctx", "fsdp"), P("fsdp", None)),
        check_vma=False,
    )
```

```python
import jax
import jax.numpy as jnp
from jax import lax
from jax.experimental import pallas as pl
from jax.experimental.pallas import tpu as pltpu
from jax.sharding import PartitionSpec as P

F32 = jnp.float32
BF16 = jnp.bfloat16
LANES = 128
PARTS = 1
FLIGHT = 2
KQ = 1
CUTX = False
ZQ = 2
DET = True
ROWS = 32


def reversed_bits(value, count):
    out = 0
    for bit in range(count):
        out |= ((value >> bit) & 1) << (count - 1 - bit)
    return out


def swap(block, axis, mask):
    size = lax.axis_size(axis)
    return lax.ppermute(block, axis, [(i, i ^ mask) for i in range(size)])


def from_behind(block, axis, distance):
    devices = range(lax.axis_size(axis))
    route = [(i - distance, i) for i in devices if i - distance in devices]
    return lax.ppermute(block, axis, route)


def lane_group(rows, per_group):
    return lax.broadcasted_iota(jnp.int32, (rows, LANES), 1) // per_group


def shifted_rows(row, taps, shift):
    wide = jnp.concatenate([row, jnp.zeros((1, taps), F32)], axis=1)
    return pltpu.roll(
        jnp.broadcast_to(wide, (taps, 2 * taps)), shift, 1, stride=1, stride_axis=0
    )


def pick_groups(stacked, taps, per_group):
    groups = LANES // per_group
    lane = lane_group(taps, per_group)
    out = stacked[:taps]
    for g in range(1, groups):
        out = jnp.where(lane == g, stacked[g * taps : (g + 1) * taps], out)
    return out


def product_kernel(k_ref, v_ref, kvp_ref):
    kvp_ref[...] = (k_ref[...].astype(F32) * v_ref[...].astype(F32)).astype(BF16)


def make_before_kernel(taps, per_group, octets):
    groups = LANES // per_group

    def kernel(f_ref, frev_ref, kvp_ref, prior_ref, z_ref, near_ref, far_ref, kvrev_ref):
        r = lax.broadcasted_iota(jnp.int32, (2 * taps, 2 * taps), 0)
        c = lax.broadcasted_iota(jnp.int32, (2 * taps, 2 * taps), 1)
        flip = jnp.where(r + c == 2 * taps - 1, 1.0, 0.0).astype(BF16)
        for o in range(octets):
            lanes = slice(o * LANES, (o + 1) * LANES)
            kv = jnp.concatenate([prior_ref[:, lanes], kvp_ref[:, lanes]], axis=0)
            rows = []
            for g in range(o * groups, (o + 1) * groups):
                toe = shifted_rows(frev_ref[g : g + 1, :], taps, 1)
                rows.append(toe.astype(BF16))
                back = shifted_rows(f_ref[g : g + 1, :], taps, 0).astype(BF16)
                near_ref[g * taps : (g + 1) * taps, :] = back[:, :taps]
                far_ref[g * taps : (g + 1) * taps, :] = back[:, taps:]
            stacked = jnp.dot(jnp.concatenate(rows, axis=0), kv, preferred_element_type=F32)
            z_ref[:, lanes] = pick_groups(stacked, taps, per_group)
            kvrev_ref[: taps - ROWS, lanes] = jnp.zeros((taps - ROWS, LANES), BF16)
            kvrev_ref[taps - ROWS :, lanes] = jnp.dot(flip, kv, preferred_element_type=F32).astype(BF16)

    return kernel


def make_pair_kernel(taps, per_group, octets):
    groups = LANES // per_group

    def kernel(gz_ref, toe_ref, kvrev_ref, gf_ref, own_ref):
        lane = lane_group(taps, per_group)
        for o in range(octets):
            lanes = slice(o * LANES, (o + 1) * LANES)
            toes = slice(o * groups * taps, (o + 1) * groups * taps)
            gz = gz_ref[:, lanes]
            stacked = jnp.dot(toe_ref[toes, :], gz, preferred_element_type=F32)
            own_ref[:, lanes] = pick_groups(stacked, taps, per_group)
            zero = jnp.zeros((ROWS, LANES), BF16)
            pairs = None
            for at in range(0, taps, ROWS):
                rows = gz[at : at + ROWS]
                split = [jnp.where(lane[:ROWS] == g, rows, zero) for g in range(groups)]
                start = taps - ROWS - at
                term = lax.dot_general(
                    jnp.concatenate(split, axis=0),
                    kvrev_ref[start : start + 2 * taps, lanes],
                    (((1,), (1,)), ((), ())),
                    preferred_element_type=F32,
                )
                pairs = term if pairs is None else pairs + term
            for g in range(groups):
                pair = pairs[g * ROWS : (g + 1) * ROWS]
                rolled = pltpu.roll(pair, taps + 1, 1, stride=1, stride_axis=0)
                row = o * groups + g
                gf_ref[row : row + 1, :] = jnp.sum(rolled[:, :taps], axis=0, keepdims=True)

    return kernel


def make_after_kernel(taps, per_group, octets):
    groups = LANES // per_group

    def kernel(later_ref, toe_ref, own_ref, k_ref, v_ref, *refs):
        gk_ref, gv_ref = refs[-2:]
        for o in range(octets):
            lanes = slice(o * LANES, (o + 1) * LANES)
            toes = slice(o * groups * taps, (o + 1) * groups * taps)
            stacked = jnp.dot(toe_ref[toes, :], later_ref[:, lanes], preferred_element_type=F32)
            grad_kv = own_ref[:, lanes] + pick_groups(stacked, taps, per_group)
            gk_ref[:, lanes] = (grad_kv * v_ref[:, lanes].astype(F32)).astype(BF16)
            gv_ref[:, lanes] = (grad_kv * k_ref[:, lanes].astype(F32)).astype(BF16)

    return kernel


def first_piece(grad_out, rows_here, e):
    n = lax.axis_size("ctx")
    nf = lax.axis_size("fsdp")
    r = n // nf
    bits = nf.bit_length() - 1
    mine = lax.axis_index("ctx")
    detour = nf // 2 if DET and (r - 1 - e) % 2 else 0
    route = []
    for i in range(n):
        for dj in range(nf):
            source = i ^ (r * dj + e)
            target = i * nf + reversed_bits(dj, bits)
            route.append((source * nf + ((i // r) ^ detour), target))
    part = (mine % r) ^ e
    cut = lax.dynamic_slice_in_dim(grad_out, part * rows_here, rows_here, axis=1)
    if detour:
        cut = swap(cut, "fsdp", detour)
    return cut, lax.ppermute(cut, ("ctx", "fsdp"), route)


def to_owner(block, q):
    n = lax.axis_size("ctx")
    nf = lax.axis_size("fsdp")
    r = n // nf
    bits = nf.bit_length() - 1
    route = []
    for i in range(n):
        for j in range(nf):
            dj = reversed_bits(j ^ q, bits)
            route.append((i * nf + j, (i ^ (r * dj)) * nf + j))
    return lax.ppermute(block, ("ctx", "fsdp"), route)


def tree_sum(values):
    while len(values) > 1:
        values = [a + b for a, b in zip(values[::2], values[1::2])]
    return values[0]


def summed_over_ctx(value, halo, after):
    n = lax.axis_size("ctx")
    steps = []
    at = 2
    while at < n:
        steps.append([k * at for k in (1, 2, 3) if k * at < n])
        at *= 4
    steps.append([1])
    for step in steps:
        sent = value.astype(BF16)
        if step == [1]:
            sent, halo = lax.optimization_barrier((sent, halo))
        got = [swap(sent, "ctx", mask) for mask in step]
        if step == [1]:
            got, after = lax.optimization_barrier((got, after))
        value = tree_sum([each.astype(F32) for each in [sent] + got])
    return value, after


def per_device(grad_out, queries, keys_in, values_in, filters, out_weight):
    n = lax.axis_size("ctx")
    nf = lax.axis_size("fsdp")
    r = n // nf
    tokens_here, channels = grad_out.shape
    group_count, taps = filters.shape
    per_group = channels // group_count
    groups = LANES // per_group
    octets = channels // LANES
    rows_here = out_weight.shape[0]
    parts = min(PARTS, octets)
    width = channels // parts
    per_part = octets // parts
    per_step = min(per_part, 8)
    steps = per_part // per_step

    kvp = pl.pallas_call(
        product_kernel,
        out_shape=jax.ShapeDtypeStruct((tokens_here, channels), BF16),
        cost_estimate=pl.CostEstimate(flops=1 << 20, bytes_accessed=64 << 20, transcendentals=0),
        name="kv_product",
    )(keys_in, values_in)
    arrived = []
    held = {"prior": from_behind(kvp, "ctx", 1)}
    pieces = {}
    cuts = {}
    for e in range(r):
        cuts[e], pieces[0, e] = first_piece(grad_out, rows_here, e)
    for e in range(r):
        for q in range(1, nf):
            low = q & -q
            piece = pieces[q ^ low, e]
            if CUTX and r > 1 and e == r - 1 and q == nf // 2:
                piece, cuts[0] = lax.optimization_barrier((piece, cuts[0]))
            pieces[q, e] = swap(piece, "fsdp", low)

    filters32 = filters.astype(F32)
    ext_rows = 3 * taps - ROWS
    lane_block = pl.BlockSpec((tokens_here, per_step * LANES), lambda o: (0, o))
    filter_block = pl.BlockSpec((per_step * groups, taps), lambda o: (o, 0))
    toe_block = pl.BlockSpec((per_step * groups * taps, taps), lambda o: (o, 0))
    ext_block = pl.BlockSpec((ext_rows, per_step * LANES), lambda o: (0, o))
    macs = channels * taps * tokens_here * groups
    params = pltpu.CompilerParams(vmem_limit_bytes=40 << 20)
    def block_sum(q, cols, earlier):
        weight = out_weight[:, cols]
        sums = {e: jnp.dot(pieces[q, e], weight, preferred_element_type=F32) for e in range(r)}
        bit = 1
        while bit < r:
            for e in [e for e in sums if e & bit]:
                sent = sums.pop(e).astype(BF16)
                if len(arrived) >= FLIGHT:
                    sent, arrived[-FLIGHT] = lax.optimization_barrier((sent, arrived[-FLIGHT]))
                got = swap(sent, "ctx", bit)
                if len(earlier) == KQ:
                    got, held["prior"] = lax.optimization_barrier((got, held["prior"]))
                arrived.append(got)
                if len(earlier) == ZQ:
                    got, earlier[0] = lax.optimization_barrier((got, earlier[0]))
                sums[e ^ bit] = sums[e ^ bit] + got.astype(F32)
            bit *= 2
        return to_owner(sums[0].astype(BF16), q)

    whole_blocks = []
    for q in range(nf - 1):
        whole_blocks.append(block_sum(q, slice(0, channels), whole_blocks))
    last_blocks = []
    for part in range(parts):
        cols = slice(part * width, (part + 1) * width)
        last_blocks.append(block_sum(nf - 1, cols, whole_blocks))
    prior = held["prior"]

    z_conv, near, far, kvrev = pl.pallas_call(
        make_before_kernel(taps, per_group, per_step),
        grid=(octets // per_step,),
        in_specs=[filter_block, filter_block, lane_block, lane_block],
        out_specs=[lane_block, toe_block, toe_block, ext_block],
        out_shape=[
            jax.ShapeDtypeStruct((tokens_here, channels), F32),
            jax.ShapeDtypeStruct((group_count * taps, taps), BF16),
            jax.ShapeDtypeStruct((group_count * taps, taps), BF16),
            jax.ShapeDtypeStruct((ext_rows, channels), BF16),
        ],
        compiler_params=params,
        cost_estimate=pl.CostEstimate(flops=4 * macs, bytes_accessed=24 << 20, transcendentals=0),
        name="forward_conv",
    )(filters32, filters32[:, ::-1], kvp, prior)

    grad_qs, terms = [], []
    grad_k = grad_v = None
    for part in range(parts):
        cols = slice(part * width, (part + 1) * width)
        owned = [block[:, cols] for block in whole_blocks] + [last_blocks[part]]
        grad_y = sum(block.astype(F32) for block in owned).astype(BF16).astype(F32)
        grad_qs.append((grad_y * z_conv[:, cols]).astype(BF16))
        grad_z = (grad_y * queries[:, cols].astype(F32)).astype(BF16)
        later = from_behind(grad_z, "ctx", -1)

        base = part * steps
        part_lanes = pl.BlockSpec((tokens_here, per_step * LANES), lambda o, b=base: (0, o + b))
        part_toes = pl.BlockSpec((per_step * groups * taps, taps), lambda o, b=base: (o + b, 0))
        part_ext = pl.BlockSpec((ext_rows, per_step * LANES), lambda o, b=base: (0, o + b))
        local_terms, own = pl.pallas_call(
            make_pair_kernel(taps, per_group, per_step),
            grid=(steps,),
            in_specs=[lane_block, part_toes, part_ext],
            out_specs=[filter_block, lane_block],
            out_shape=[
                jax.ShapeDtypeStruct((group_count // parts, taps), F32),
                jax.ShapeDtypeStruct((tokens_here, width), F32),
            ],
            compiler_params=params,
            cost_estimate=pl.CostEstimate(
                flops=4 * macs // parts, bytes_accessed=(12 << 20) // parts, transcendentals=0
            ),
            name="pair_products",
        )(grad_z, near, kvrev)
        terms.append(local_terms)

        earlier = [] if part == 0 else [grad_k, grad_v]
        plane16 = jax.ShapeDtypeStruct((tokens_here, channels), BF16)
        grad_k, grad_v = pl.pallas_call(
            make_after_kernel(taps, per_group, per_step),
            grid=(steps,),
            in_specs=[lane_block, part_toes, lane_block, part_lanes, part_lanes]
            + [pl.BlockSpec(memory_space=pl.ANY)] * len(earlier),
            out_specs=[part_lanes, part_lanes],
            out_shape=[plane16, plane16],
            input_output_aliases={5 + at: at for at in range(len(earlier))},
            compiler_params=params,
            cost_estimate=pl.CostEstimate(
                flops=2 * macs // parts, bytes_accessed=(8 << 20) // parts, transcendentals=0
            ),
            name="backward_conv",
        )(later, far, own, keys_in, values_in, *earlier)

    grad_filters, (grad_k, grad_v) = summed_over_ctx(jnp.concatenate(terms, axis=0), later, (grad_k, grad_v))
    return (jnp.concatenate(grad_qs, axis=1), grad_k, grad_v, grad_filters)


def solution(mesh):
    placed = (
        P("ctx", "fsdp"),
        P("ctx", "fsdp"),
        P("ctx", "fsdp"),
        P("ctx", "fsdp"),
        P("fsdp", None),
        P("ctx", "fsdp"),
    )
    return jax.shard_map(
        per_device,
        mesh=mesh,
        in_specs=placed,
        out_specs=(P("ctx", "fsdp"), P("ctx", "fsdp"), P("ctx", "fsdp"), P("fsdp", None)),
        check_vma=False,
    )
```
